256 devices in a mesh: dp: 32 (over y_hi, z, core), tensor: 8 (over y_lo, x).
Axes of the slice: x: 4, y: 4 (y_hi: 2, y_lo: 2; y = y_hi * 2 + y_lo), z: 8, core: 2. Of those that a mesh axis runs over, the one named last changes fastest.
Arguments:
- tokens: bfloat16 [16384, 3072], P('dp', 'tensor'), may hold values from -6 to 6
- w_in: bfloat16 [3072, 12288], P('dp', 'tensor'), may hold values from -0.109375 to 0.109375
- cotangent: bfloat16 [16384, 12288], P('dp', 'tensor'), may hold values from -6 to 6
Outputs:
- hidden: bfloat16 [16384, 12288], P('dp', 'tensor')
- x_grad: bfloat16 [16384, 3072], P('dp', 'tensor')
- w_grad: bfloat16 [3072, 12288], P('dp', 'tensor')
The draws below stay inside these ranges and needn't reach their ends.
All inputs are finite; a program needn't handle non-finite values.
Results may differ from the reference program's by a relative error of at most 0.028.
Values may be sent and summed in bfloat16 or wider, within the bound.
No kernel may reach another device: no remote copies, remote signals or barrier semaphores. Data moves between devices by JAX's collectives and lax.ppermute only.
A program may use at most 128 MiB of HBM per device.

```python
import jax
import jax.numpy as jnp
from jax import lax

D = 3072
FF_DEV = 1536
TOK_DEV = 512
FF = 12288
TOKENS = 16384
N_DP = 32
N_TENSOR = 8


def with_spikes(array, stream_key, source, target, parts, factor):
    def block_of(position):
        return (jnp.arange(array.shape[position]) // (array.shape[position] // parts)).reshape((-1,) + (1,) * (array.ndim - 1 - position))

    first = jax.random.permutation(stream_key, parts)[block_of(target)]
    second = (block_of(target) + parts // 2) % parts
    return jnp.where((block_of(source) == first) | (block_of(source) == second), factor * array, array)


def level_of(key, shape, split, low, high):
    loudness = 1.0
    for position, blocks in split:
        steps = jax.random.uniform(jax.random.fold_in(jax.random.fold_in(key, 6), position), (blocks,), jnp.float32, low / len(split), high / len(split))
        loudness = loudness * jnp.repeat(jnp.exp(steps), shape[position] // blocks).reshape((-1,) + (1,) * (len(shape) - 1 - position))
    return loudness


def normal_values(stream_key, shape, spread, most, pieces=(), kind=jnp.bfloat16):
    entries = spread * jax.random.normal(stream_key, shape, jnp.float32)
    if pieces:
        entries = entries * level_of(stream_key, shape, pieces, -0.22, 0.18)
    return jnp.clip(entries, -most, most).astype(kind)


def noise_with(key, extent, scale, limit, pieces, heavy, kind=jnp.bfloat16):
    entries = scale * jax.random.normal(key, extent, jnp.float32)
    if pieces:
        entries = entries * level_of(key, extent, pieces, -0.22, 0.18)
    return jnp.clip(with_spikes(entries, jax.random.fold_in(key, 3), *heavy), -limit, limit).astype(kind)


def setup_inputs(seed: int = 0) -> dict:
    streams_of = jax.random.split(jax.random.key(seed), 4)
    tokens = noise_with(streams_of[0], (TOKENS, D), 1.0, 6.0, ((0, 32), (1, 8)), (0, 1, 32, 2.75))
    w_in = normal_values(streams_of[1], (D, FF), D ** -0.5, 0.109375, ((0, 32), (1, 8)))
    cotangent = normal_values(streams_of[2], (TOKENS, FF), 1.0, 6.0, ((0, 32), (1, 8)))
    return dict(tokens=tokens, w_in=w_in, cotangent=cotangent)


def gelu_tanh(values):
    return jax.nn.gelu(values, approximate=True)

def reference(tokens, w_in, cotangent):
    row_groups = tokens.reshape(N_DP, TOK_DEV, D)
    cot_groups = cotangent.reshape(N_DP, TOK_DEV, FF)

    def accumulate(running, pair):
        row_block, cot_block = pair
        preact = jnp.dot(row_block, w_in, preferred_element_type=jnp.float32)
        activ, pull_back = jax.vjp(gelu_tanh, preact)
        pre_grad = pull_back(cot_block.astype(jnp.float32))[0].astype(jnp.bfloat16)
        input_grad = jnp.zeros((TOK_DEV, D), jnp.float32)
        for group in range(N_TENSOR):
            grad_cols = pre_grad[:, group * FF_DEV:(group + 1) * FF_DEV]
            weight_cols = w_in[:, group * FF_DEV:(group + 1) * FF_DEV]
            piece = lax.dot_general(grad_cols, weight_cols, (((1,), (1,)), ((), ())), preferred_element_type=jnp.float32)
            piece = lax.optimization_barrier(piece.astype(jnp.bfloat16)).astype(jnp.float32)
            input_grad = input_grad + piece
        partial_value = lax.dot_general(row_block, pre_grad, (((0,), (0,)), ((), ())), preferred_element_type=jnp.float32)
        partial_value = lax.optimization_barrier(partial_value.astype(jnp.bfloat16)).astype(jnp.float32)
        return (running + partial_value, (activ.astype(jnp.bfloat16), input_grad.astype(jnp.bfloat16)))
    start = jnp.zeros((D, FF), jnp.float32)
    summed, (hidden, x_grad) = lax.scan(accumulate, start, (row_groups, cot_groups))
    return (hidden.reshape(TOKENS, FF), x_grad.reshape(TOKENS, D), summed.astype(jnp.bfloat16))
```

```python
import jax
import jax.numpy as jnp
from jax import lax
from jax.sharding import Mesh, PartitionSpec as P

F32, BF16 = jnp.float32, jnp.bfloat16
AXES = ("yh", "z", "core", "yl", "x")
SIZES = (2, 8, 2, 2, 4)


def gelu_tanh(values):
    return jax.nn.gelu(values, approximate=True)


def shift(block, axis, step):
    count = SIZES[AXES.index(axis)]
    return lax.ppermute(block, axis, [(i, (i + step) % count) for i in range(count)])


def ordered(index, own, other):
    return jnp.where(index == 0, jnp.stack([own, other]), jnp.stack([other, own]))


def gather_tokens(tok):
    own = tok.T
    pair = ordered(lax.axis_index("yl"), own, shift(own, "yl", 1))
    ahead, behind = shift(pair, "x", 1), shift(pair, "x", -1)
    opposite = jnp.stack([shift(ahead[0], "x", 1), shift(behind[1], "x", -1)])
    x = lax.axis_index("x")
    out = jnp.zeros((2, 4, 384, 512), BF16)
    for block, at in ((pair, x), (ahead, (x + 3) % 4), (behind, (x + 1) % 4), (opposite, (x + 2) % 4)):
        out = lax.dynamic_update_slice(out, block[:, None], (0, at, 0, 0))
    return out


def gather_weights(w):
    z, core = lax.axis_index("z"), lax.axis_index("core")
    pair = ordered(lax.axis_index("yh"), w, shift(w, "yh", 1))
    blocks = [(pair, z)]
    ahead = behind = pair
    for k in range(1, 4):
        ahead, behind = shift(ahead, "z", 1), shift(behind, "z", -1)
        blocks += [(ahead, (z + 8 - k) % 8), (behind, (z + k) % 8)]
    opposite = jnp.stack([shift(ahead[0], "z", 1), shift(behind[1], "z", -1)])
    blocks.append((opposite, (z + 4) % 8))
    out = jnp.zeros((2, 8, 2, 96, 1536), BF16)
    for block, at in blocks:
        swapped = shift(block, "core", 1)
        out = lax.dynamic_update_slice(out, block[:, None, None], (0, at, core, 0, 0))
        out = lax.dynamic_update_slice(out, swapped[:, None, None], (0, at, 1 - core, 0, 0))
    return out


def scatter_sum(part, axis, halves):
    count = SIZES[AXES.index(axis)]
    ahead, behind = halves(part(count // 2))
    ahead, behind = ahead.astype(BF16), behind.astype(BF16)
    ahead, behind = shift(ahead, axis, 1), shift(behind, axis, -1)
    first = True
    for k in range(count // 2 - 1, 0, -1):
        up, down = part(k), part(count - k)
        if first:
            a, b = halves(up)
            up = jnp.concatenate([a + ahead.astype(F32), b], 0)
            a, b = halves(down)
            down = jnp.concatenate([a, b + behind.astype(F32)], 0)
            first = False
        else:
            up, down = up + ahead.astype(F32), down + behind.astype(F32)
        ahead, behind = shift(up.astype(BF16), axis, 1), shift(down.astype(BF16), axis, -1)
    return part(0) + ahead.astype(F32) + behind.astype(F32)


def halves(block):
    return block[:1], block[1:]


def on_device(tok, w, cot):
    yh, z, core, yl, x = (lax.axis_index(a) for a in AXES)
    tokens_t = gather_tokens(tok).reshape(2, 8, 2, 96, 512)
    weights = gather_weights(w)
    flat = weights.reshape(3072, 1536)
    preact = lax.dot_general(
        tokens_t.reshape(3072, 512), flat, (((0,), (0,)), ((), ())), preferred_element_type=F32
    )
    hidden = gelu_tanh(preact).astype(BF16)
    pull_back = jax.vjp(gelu_tanh, preact)[1]
    pre_grad = pull_back(cot.astype(F32))[0].astype(BF16)

    mine = lax.dynamic_index_in_dim(tokens_t, core, 2, keepdims=False)
    theirs = lax.dynamic_index_in_dim(tokens_t, 1 - core, 2, keepdims=False)
    both_tokens = jnp.concatenate([mine, shift(theirs, "core", 1)], axis=-1)
    both_grads = jnp.concatenate([pre_grad, shift(pre_grad, "core", 1)], axis=0)

    def w_part(k):
        rows = lax.dynamic_index_in_dim(both_tokens, (z + k) % 8, 1, keepdims=False)
        return jnp.dot(rows.reshape(192, 1024), both_grads, preferred_element_type=F32).reshape(2, 96, 1536)

    w_sum = scatter_sum(w_part, "z", halves)
    keep = lax.dynamic_index_in_dim(w_sum, yh, 0, keepdims=False)
    give = lax.dynamic_index_in_dim(w_sum, 1 - yh, 0, keepdims=False).astype(BF16)
    w_grad = (keep + shift(give, "yh", 1).astype(F32)).astype(BF16)

    by_x = weights.reshape(2, 4, 384, 1536)

    def x_part(k):
        rows = lax.dynamic_index_in_dim(by_x, (x + k) % 4, 1, keepdims=False)
        return lax.dot_general(
            rows, pre_grad, (((2,), (1,)), ((), ())), preferred_element_type=F32
        )

    x_sum = scatter_sum(x_part, "x", halves)
    keep = lax.dynamic_index_in_dim(x_sum, yl, 0, keepdims=False)
    give = lax.dynamic_index_in_dim(x_sum, 1 - yl, 0, keepdims=False).astype(BF16)
    x_grad = (keep + shift(give, "yl", 1).astype(F32)).astype(BF16).T
    return hidden, x_grad, w_grad


def solution(mesh):
    fine = Mesh(mesh.devices.reshape(SIZES), AXES)
    spec = P(("yh", "z", "core"), ("yl", "x"))
    return jax.shard_map(
        on_device, mesh=fine, in_specs=(spec,) * 3, out_specs=(spec,) * 3, check_vma=False
    )
```

```python
import jax
import jax.numpy as jnp
from jax import lax
from jax.sharding import Mesh, PartitionSpec as P

F32, BF16 = jnp.float32, jnp.bfloat16
AXES = ("yh", "z", "core", "yl", "x")
SIZES = (2, 8, 2, 2, 4)


def gelu_tanh(values):
    return jax.nn.gelu(values, approximate=True)


def swap(block, axis):
    return lax.ppermute(block, axis, [(0, 1), (1, 0)])


def ring(block, axis):
    count = SIZES[AXES.index(axis)]
    place = (lambda i, c: 2 * i + c) if axis == "z" else (lambda i, c: count * c + i)
    hops = [(place(i, c), place((i + 1 - 2 * c) % count, c)) for i in range(count) for c in range(2)]
    return lax.ppermute(block, ("z", "core") if axis == "z" else ("core", "x"), hops)


def shift(block, axis, step):
    count = SIZES[AXES.index(axis)]
    return lax.ppermute(block, axis, [(i, (i + step) % count) for i in range(count)])


def dot(left, right, left_dim, right_dim):
    return lax.dot_general(
        left, right, (((left_dim,), (right_dim,)), ((), ())), preferred_element_type=F32
    )


def later(array, other):
    corner = lax.slice(other, (0,) * other.ndim, (1,) * other.ndim).reshape(()).astype(F32)
    return array + (0.0 * corner).astype(array.dtype)


def plus(part, received):
    return (part + received.astype(F32)).astype(BF16)


def on_device(tok, w, cot):
    yh, z, core, yl, x = (lax.axis_index(a) for a in AXES)
    sign = 1 - 2 * core

    def spot_z(other, ahead):
        return (yh + other) % 2, (z + 8 + sign * ahead) % 8

    def spot_x(other, ahead):
        return (yl + other) % 2, (x + 4 + sign * ahead) % 4

    def chip_rows(rows):
        got = swap(rows, "core")
        return jnp.where(core == 0, jnp.concatenate([rows, got], 0), jnp.concatenate([got, rows], 0))

    weights = jnp.zeros((2, 8, 192, 1536), BF16)

    def place_w(buffer, block, other, ahead):
        return lax.dynamic_update_slice(buffer, block[None, None], (*spot_z(other, ahead), 0, 0))

    across = swap(w, "yh")
    a, b = chip_rows(w), chip_rows(across)
    weights = place_w(place_w(weights, a, 0, 0), b, 1, 0)
    for k in range(1, 4):
        a = ring(a, "z")
        weights = place_w(place_w(weights, a, 0, -k), swap(a, "core"), 0, k)
        b = ring(b, "z")
        weights = place_w(place_w(weights, b, 1, -k), swap(b, "core"), 1, k)
    far = ring(jnp.where(core == 0, a, b), "z")
    weights = place_w(place_w(weights, far, core, 4), swap(far, "core"), 1 - core, 4)

    tokens, both = jnp.zeros((2, 4, 384, 512), BF16), jnp.zeros((2, 8, 96, 1024), BF16)

    def place_t(buffers, block, other, ahead, turned):
        row, column = spot_x(other, ahead)
        halves = (block[:, 512:], block[:, :512]) if turned else (block[:, :512], block[:, 512:])
        few = lax.dynamic_index_in_dim(block.reshape(2, 2, 96, 1024), core, 1, keepdims=False)
        pieces = [(few[:, :, 512:], 0), (few[:, :, :512], 512)] if turned else [(few, 0)]
        out = lax.dynamic_update_slice(buffers[0], halves[0][None, None], (row, column, 0, 0))
        part = buffers[1]
        for piece, lane in pieces:
            part = lax.dynamic_update_slice(part, piece[None], (row, 2 * column, 0, lane))
        return out, part

    t_own = tok.T
    t_other = swap(later(t_own, across), "yl")
    a = jnp.concatenate([t_own, swap(t_own, "core")], 1)
    b = jnp.concatenate([t_other, swap(t_other, "core")], 1)
    known = place_t(place_t((tokens, both), a, 0, 0, False), b, 1, 0, False)
    a, b = ring(a, "x"), ring(b, "x")
    known = place_t(place_t(known, a, 0, -1, False), swap(a, "core"), 0, 1, True)
    known = place_t(place_t(known, b, 1, -1, False), swap(b, "core"), 1, 1, True)
    far = ring(jnp.where(core == 0, a, b), "x")
    known = place_t(place_t(known, far, core, 2, False), swap(far, "core"), 1 - core, 2, True)

    tokens, both = known
    preact = dot(tokens.reshape(3072, 512), weights.reshape(3072, 1536), 0, 0)
    hidden = gelu_tanh(preact).astype(BF16)
    pull_back = jax.vjp(gelu_tanh, preact)[1]
    grad = pull_back(cot.astype(F32))[0].astype(BF16)
    grads = jnp.concatenate([grad, swap(grad, "core")], 0)

    def w_part(ahead):
        rows = lax.dynamic_index_in_dim(both, (z + 8 + ahead) % 8, 1, keepdims=False)
        return dot(rows.reshape(192, 1024), grads, 1, 0).reshape(2, 96, 1536)

    def pick(array, index, other):
        return lax.dynamic_index_in_dim(array, (index + other) % 2, 0, keepdims=False)

    far = gate = w_part(4).astype(BF16)
    up, down = shift(far[0], "z", 1), shift(far[1], "z", -1)
    part = w_part(3)
    up = jnp.stack([plus(part[0], up), part[1].astype(BF16)])
    part = w_part(-3)
    down = jnp.stack([part[0].astype(BF16), plus(part[1], down)])
    up, down = shift(up, "z", 1), shift(down, "z", -1)
    up, down = plus(w_part(2), up), plus(w_part(-2), down)
    up, down = shift(up, "z", 1), shift(down, "z", -1)
    up, down = plus(w_part(1), up), plus(w_part(-1), down)
    home = w_part(0)
    b_up, b_down = shift(pick(up, yh, 1), "z", 1), shift(pick(down, yh, 1), "z", -1)
    a_up, a_down = shift(pick(up, yh, 0), "z", 1), shift(pick(down, yh, 0), "z", -1)
    b = swap(plus(pick(home, yh, 1) + b_up.astype(F32), b_down), "yh")
    w_grad = plus(pick(home, yh, 0) + a_up.astype(F32) + a_down.astype(F32), b)

    by_x = weights.reshape(2, 4, 384, 1536)

    def x_part(ahead):
        rows = lax.dynamic_index_in_dim(by_x, (x + 4 + ahead) % 4, 1, keepdims=False)
        return later(dot(rows, grad, 2, 1), gate).astype(BF16)

    far = x_part(2)
    up, down = shift(far[0], "x", 1), shift(far[1], "x", -1)
    part = x_part(1)
    up = jnp.stack([plus(part[0].astype(F32), up), part[1]])
    part = x_part(-1)
    down = jnp.stack([part[0], plus(part[1].astype(F32), down)])
    up, down = shift(up, "x", 1), shift(down, "x", -1)
    x_sum = x_part(0).astype(F32) + up.astype(F32) + down.astype(F32)
    x_grad = plus(pick(x_sum, yl, 0), swap(pick(x_sum, yl, 1).astype(BF16), "yl")).T
    return hidden, x_grad, w_grad


def solution(mesh):
    fine = Mesh(mesh.devices.reshape(SIZES), AXES)
    spec = P(("yh", "z", "core"), ("yl", "x"))
    return jax.shard_map(
        on_device, mesh=fine, in_specs=(spec,) * 3, out_specs=(spec,) * 3, check_vma=False
    )
```

```python
import jax
import jax.numpy as jnp
from jax import lax
from jax.sharding import Mesh, PartitionSpec as P

F32, BF16 = jnp.float32, jnp.bfloat16
AXES = ("yh", "z", "core", "yl", "x")
SIZES = (2, 8, 2, 2, 4)


def gelu_tanh(values):
    return jax.nn.gelu(values, approximate=True)


def swap(block, axis):
    return lax.ppermute(block, axis, [(0, 1), (1, 0)])


def ring(block, axis):
    count = SIZES[AXES.index(axis)]
    place = (lambda i, c: 2 * i + c) if axis == "z" else (lambda i, c: count * c + i)
    hops = [(place(i, c), place((i + 1 - 2 * c) % count, c)) for i in range(count) for c in range(2)]
    return lax.ppermute(block, ("z", "core") if axis == "z" else ("core", "x"), hops)


def shift(block, axis, step):
    count = SIZES[AXES.index(axis)]
    return lax.ppermute(block, axis, [(i, (i + step) % count) for i in range(count)])


def dot(left, right, left_dim, right_dim):
    return lax.dot_general(
        left, right, (((left_dim,), (right_dim,)), ((), ())), preferred_element_type=F32
    )


def later(array, other):
    across = array.shape[-1] <= other.shape[-1]
    size = (1, array.shape[-1]) if across else (array.shape[-2], 1)
    edge = lax.slice(other, (0,) * other.ndim, (1,) * (other.ndim - 2) + size).reshape(size)
    return array + (0.0 * edge.astype(F32)).astype(array.dtype)


def plus(part, received):
    return (part + received.astype(F32)).astype(BF16)


def on_device(tok, w, cot):
    yh, z, core, yl, x = (lax.axis_index(a) for a in AXES)
    sign = 1 - 2 * core

    def spot_z(other, ahead):
        return (yh + other) % 2, (z + 8 + sign * ahead) % 8

    def spot_x(other, ahead):
        return (yl + other) % 2, (x + 4 + sign * ahead) % 4

    def chip_rows(rows):
        got = swap(rows, "core")
        return jnp.where(core == 0, jnp.concatenate([rows, got], 0), jnp.concatenate([got, rows], 0))

    weights = jnp.zeros((2, 8, 192, 1536), BF16)

    def place_w(buffer, block, other, ahead):
        return lax.dynamic_update_slice(buffer, block[None, None], (*spot_z(other, ahead), 0, 0))

    across = swap(w, "yh")
    a = chip_rows(w)
    t_own = tok.T
    t_pair = jnp.concatenate([t_own, swap(t_own, "core")], 1)
    b = chip_rows(later(later(across, a), t_pair))
    t_other = later(swap(later(t_own, a), "yl"), b)
    weights = place_w(place_w(weights, a, 0, 0), b, 1, 0)
    for k in range(1, 4):
        a = ring(a, "z")
        weights = place_w(place_w(weights, a, 0, -k), swap(a, "core"), 0, k)
        b = ring(b, "z")
        weights = place_w(place_w(weights, b, 1, -k), swap(b, "core"), 1, k)
    last = ring(jnp.where(core == 0, a, b), "z")

    tokens, both = jnp.zeros((2, 4, 384, 512), BF16), jnp.zeros((2, 8, 96, 1024), BF16)

    def place_t(buffers, block, other, ahead, turned):
        row, column = spot_x(other, ahead)
        halves = (block[:, 512:], block[:, :512]) if turned else (block[:, :512], block[:, 512:])
        few = lax.dynamic_index_in_dim(block.reshape(2, 2, 96, 1024), core, 1, keepdims=False)
        pieces = [(few[:, :, 512:], 0), (few[:, :, :512], 512)] if turned else [(few, 0)]
        out = lax.dynamic_update_slice(buffers[0], halves[0][None, None], (row, column, 0, 0))
        part = buffers[1]
        for piece, lane in pieces:
            part = lax.dynamic_update_slice(part, piece[None], (row, 2 * column, 0, lane))
        return out, part

    a = t_pair
    b = jnp.concatenate([t_other, swap(t_other, "core")], 1)
    known = place_t(place_t((tokens, both), a, 0, 0, False), b, 1, 0, False)
    a, b = ring(a, "x"), ring(b, "x")
    known = place_t(place_t(known, a, 0, -1, False), swap(a, "core"), 0, 1, True)
    known = place_t(place_t(known, b, 1, -1, False), swap(b, "core"), 1, 1, True)
    far = ring(jnp.where(core == 0, a, b), "x")
    known = place_t(place_t(known, far, core, 2, False), swap(far, "core"), 1 - core, 2, True)

    tokens, both = known
    preact = dot(tokens.reshape(3072, 512), weights.reshape(3072, 1536), 0, 0)
    by_z = tokens.reshape(2, 8, 192, 512)
    last = later(last, preact)
    for block, other in ((last, core), (swap(last, "core"), 1 - core)):
        rows = lax.dynamic_slice(by_z, (*spot_z(other, 4), 0, 0), (1, 1, 192, 512))
        preact = preact + dot(rows.reshape(192, 512), block, 0, 0)
        weights = place_w(weights, block, other, 4)
    hidden = gelu_tanh(preact).astype(BF16)
    pull_back = jax.vjp(gelu_tanh, preact)[1]
    grad = pull_back(cot.astype(F32))[0].astype(BF16)
    grad_other = swap(grad, "core")
    grads = jnp.concatenate([grad, grad_other], 0)

    def w_part(other, ahead):
        start = (*((yh + other) % 2, (z + 8 + ahead) % 8), 0, 0)
        return dot(lax.dynamic_slice(both, start, (1, 1, 96, 1024)).reshape(96, 1024), grads, 1, 0)

    def pick(array, index, other):
        return lax.dynamic_index_in_dim(array, (index + other) % 2, 0, keepdims=False)

    b_far = w_part(1, 4).astype(BF16)
    b_up, b_down = w_part(1, 3).astype(BF16), w_part(1, -3).astype(BF16)
    gate = b_down
    b_up, b_down = shift(b_up, "z", 1), shift(b_down, "z", -1)
    b_far = swap(b_far, "yh")
    a_far = plus(w_part(0, 4), b_far)
    a_up, a_down = shift(a_far[:48], "z", 1), shift(a_far[48:], "z", -1)
    gate_near = a_down
    for k in range(3, 0, -1):
        if k < 3:
            b_up = shift(plus(w_part(1, k), b_up), "z", 1)
            b_down = shift(plus(w_part(1, -k), b_down), "z", -1)
            up, down = plus(w_part(0, k), a_up), plus(w_part(0, -k), a_down)
        else:
            up, down = w_part(0, k), w_part(0, -k)
            up = jnp.concatenate([plus(up[:48], a_up), up[48:].astype(BF16)], 0)
            down = jnp.concatenate([down[:48].astype(BF16), plus(down[48:], a_down)], 0)
        a_up, a_down = shift(up, "z", 1), shift(down, "z", -1)
    b_sum = plus(w_part(1, 0) + b_up.astype(F32), b_down)
    a_sum = w_part(0, 0) + a_up.astype(F32) + a_down.astype(F32)
    w_grad = plus(a_sum, swap(b_sum, "yh"))

    by_x = weights.reshape(2, 4, 384, 1536)

    def x_part(ahead, gate):
        rows = lax.dynamic_index_in_dim(by_x, (x + 4 + ahead) % 4, 1, keepdims=False)
        return later(dot(rows, grad, 2, 1), gate).astype(BF16)

    far = x_part(2, gate)
    up, down = shift(far[0], "x", 1), shift(far[1], "x", -1)
    part = x_part(1, gate_near)
    up = jnp.stack([plus(part[0].astype(F32), up), part[1]])
    part = x_part(-1, gate_near)
    down = jnp.stack([part[0], plus(part[1].astype(F32), down)])
    up, down = shift(up, "x", 1), shift(down, "x", -1)
    x_sum = x_part(0, gate_near).astype(F32) + up.astype(F32) + down.astype(F32)
    x_grad = plus(pick(x_sum, yl, 0), swap(pick(x_sum, yl, 1).astype(BF16), "yl")).T
    return hidden, x_grad, w_grad


def solution(mesh):
    fine = Mesh(mesh.devices.reshape(SIZES), AXES)
    spec = P(("yh", "z", "core"), ("yl", "x"))
    return jax.shard_map(
        on_device, mesh=fine, in_specs=(spec,) * 3, out_specs=(spec,) * 3, check_vma=False
    )
```

```python
import jax
import jax.numpy as jnp
from jax import lax
from jax.sharding import Mesh, PartitionSpec as P

F32, BF16 = jnp.float32, jnp.bfloat16
AXES = ("yh", "z", "core", "yl", "x")
SIZES = (2, 8, 2, 2, 4)


def gelu_tanh(values):
    return jax.nn.gelu(values, approximate=True)


def swap(block, axis):
    return lax.ppermute(block, axis, [(0, 1), (1, 0)])


def ring(block, axis):
    count = SIZES[AXES.index(axis)]
    place = (lambda i, c: 2 * i + c) if axis == "z" else (lambda i, c: count * c + i)
    hops = [(place(i, c), place((i + 1 - 2 * c) % count, c)) for i in range(count) for c in range(2)]
    return lax.ppermute(block, ("z", "core") if axis == "z" else ("core", "x"), hops)


def shift(block, axis, step):
    count = SIZES[AXES.index(axis)]
    return lax.ppermute(block, axis, [(i, (i + step) % count) for i in range(count)])


def dot(left, right, left_dim, right_dim):
    return lax.dot_general(
        left, right, (((left_dim,), (right_dim,)), ((), ())), preferred_element_type=F32
    )


def later(array, other):
    across = array.shape[-1] <= other.shape[-1]
    size = (1, array.shape[-1]) if across else (array.shape[-2], 1)
    edge = lax.slice(other, (0,) * other.ndim, (1,) * (other.ndim - 2) + size).reshape(size)
    return array + (0.0 * edge.astype(F32)).astype(array.dtype)


def plus(part, received):
    return (part + received.astype(F32)).astype(BF16)


def on_device(tok, w, cot):
    yh, z, core, yl, x = (lax.axis_index(a) for a in AXES)
    sign = 1 - 2 * core

    def spot_z(other, ahead):
        return (yh + other) % 2, (z + 8 + sign * ahead) % 8

    def spot_x(other, ahead):
        return (yl + other) % 2, (x + 4 + sign * ahead) % 4

    def chip_rows(rows):
        got = swap(rows, "core")
        return jnp.where(core == 0, jnp.concatenate([rows, got], 0), jnp.concatenate([got, rows], 0))

    weights = jnp.zeros((2, 8, 192, 1536), BF16)

    def place_w(buffer, block, other, ahead):
        return lax.dynamic_update_slice(buffer, block[None, None], (*spot_z(other, ahead), 0, 0))

    across = swap(w, "yh")
    a = chip_rows(w)
    t_own = tok.T
    t_pair = jnp.concatenate([t_own, swap(t_own, "core")], 1)
    b = chip_rows(later(across, a))
    t_other = swap(later(t_own, a), "yl")
    weights = place_w(place_w(weights, a, 0, 0), b, 1, 0)
    for k in range(1, 4):
        a = ring(a, "z")
        if k == 1:
            t_other = later(t_other, a)
        weights = place_w(place_w(weights, a, 0, -k), swap(a, "core"), 0, k)
        b = ring(b, "z")
        weights = place_w(place_w(weights, b, 1, -k), swap(b, "core"), 1, k)
    last = ring(jnp.where(core == 0, a, b), "z")

    tokens, both = jnp.zeros((2, 4, 384, 512), BF16), jnp.zeros((2, 8, 96, 1024), BF16)

    def place_t(buffers, block, other, ahead, turned):
        row, column = spot_x(other, ahead)
        halves = (block[:, 512:], block[:, :512]) if turned else (block[:, :512], block[:, 512:])
        few = lax.dynamic_index_in_dim(block.reshape(2, 2, 96, 1024), core, 1, keepdims=False)
        pieces = [(few[:, :, 512:], 0), (few[:, :, :512], 512)] if turned else [(few, 0)]
        out = lax.dynamic_update_slice(buffers[0], halves[0][None, None], (row, column, 0, 0))
        part = buffers[1]
        for piece, lane in pieces:
            part = lax.dynamic_update_slice(part, piece[None], (row, 2 * column, 0, lane))
        return out, part

    a = t_pair
    b = jnp.concatenate([t_other, swap(t_other, "core")], 1)
    known = place_t(place_t((tokens, both), a, 0, 0, False), b, 1, 0, False)
    a, b = ring(a, "x"), ring(b, "x")
    known = place_t(place_t(known, a, 0, -1, False), swap(a, "core"), 0, 1, True)
    known = place_t(place_t(known, b, 1, -1, False), swap(b, "core"), 1, 1, True)
    far = ring(jnp.where(core == 0, a, b), "x")
    known = place_t(place_t(known, far, core, 2, False), swap(far, "core"), 1 - core, 2, True)

    tokens, both = known
    preact = dot(tokens.reshape(3072, 512), weights.reshape(3072, 1536), 0, 0)
    by_z = tokens.reshape(2, 8, 192, 512)
    last = later(last, preact)
    for block, other in ((last, core), (swap(last, "core"), 1 - core)):
        rows = lax.dynamic_slice(by_z, (*spot_z(other, 4), 0, 0), (1, 1, 192, 512))
        preact = preact + dot(rows.reshape(192, 512), block, 0, 0)
        weights = place_w(weights, block, other, 4)
    hidden = gelu_tanh(preact).astype(BF16)
    pull_back = jax.vjp(gelu_tanh, preact)[1]
    grad = pull_back(cot.astype(F32))[0].astype(BF16)
    grad_other = swap(grad, "core")
    grads = jnp.concatenate([grad, grad_other], 0)

    def w_part(other, ahead):
        start = (*((yh + other) % 2, (z + 8 + ahead) % 8), 0, 0)
        return dot(lax.dynamic_slice(both, start, (1, 1, 96, 1024)).reshape(96, 1024), grads, 1, 0)

    def pick(array, index, other):
        return lax.dynamic_index_in_dim(array, (index + other) % 2, 0, keepdims=False)

    by_x = weights.reshape(2, 4, 384, 1536)

    def x_part(ahead, *gates):
        rows = lax.dynamic_index_in_dim(by_x, (x + 4 + ahead) % 4, 1, keepdims=False)
        part = dot(rows, grad, 2, 1)
        for gate in gates:
            part = later(part, gate)
        return part.astype(BF16)

    far = ring(x_part(2), "x")

    b_far = w_part(1, 4).astype(BF16)
    b_up, b_down = w_part(1, 3).astype(BF16), w_part(1, -3).astype(BF16)
    b_up, b_down = shift(b_up, "z", 1), shift(b_down, "z", -1)
    b_far = swap(b_far, "yh")
    a_far = plus(w_part(0, 4), b_far)
    near_up, near_down = x_part(1, a_far), x_part(-1, a_far)
    a_far = ring(a_far, "z")
    for k in range(3, 0, -1):
        if k < 3:
            b_up, b_down = plus(w_part(1, k), b_up), plus(w_part(1, -k), b_down)
            if k == 2:
                b_up, b_down = later(b_up, near_up), later(b_down, near_down)
                gate_far = b_up
            b_up, b_down = shift(b_up, "z", 1), shift(b_down, "z", -1)
            up, down = plus(w_part(0, k), a_up), plus(w_part(0, -k), a_down)
        else:
            up = plus(w_part(0, k), jnp.where(core == 0, a_far, 0))
            down = plus(w_part(0, -k), jnp.where(core == 1, a_far, 0))
        a_up, a_down = shift(up, "z", 1), shift(down, "z", -1)
        gate_home = a_down if k == 3 else gate_home
    b_sum = plus(w_part(1, 0) + b_up.astype(F32), b_down)
    a_sum = w_part(0, 0) + a_up.astype(F32) + a_down.astype(F32)
    w_grad = plus(a_sum, swap(b_sum, "yh"))

    far = later(far, gate_far)

    def with_far(part, index):
        far_here = jnp.where(core == index, far, 0)
        return jnp.stack([plus(part[i].astype(F32), far_here[i]) for i in range(2)])

    up, down = with_far(near_up, 0), with_far(near_down, 1)
    up, down = shift(up, "x", 1), shift(down, "x", -1)
    x_sum = x_part(0, gate_home).astype(F32) + up.astype(F32) + down.astype(F32)
    x_grad = plus(pick(x_sum, yl, 0), swap(pick(x_sum, yl, 1).astype(BF16), "yl")).T
    return hidden, x_grad, w_grad


def solution(mesh):
    fine = Mesh(mesh.devices.reshape(SIZES), AXES)
    spec = P(("yh", "z", "core"), ("yl", "x"))
    return jax.shard_map(
        on_device, mesh=fine, in_specs=(spec,) * 3, out_specs=(spec,) * 3, check_vma=False
    )
```

```python
import jax
import jax.numpy as jnp
from jax import lax
from jax.sharding import Mesh, PartitionSpec as P

F32, BF16 = jnp.float32, jnp.bfloat16
AXES = ("yh", "z", "core", "yl", "x")
SIZES = (2, 8, 2, 2, 4)


def gelu_tanh(values):
    return jax.nn.gelu(values, approximate=True)


def swap(block, axis):
    return lax.ppermute(block, axis, [(0, 1), (1, 0)])


def ring(block, axis):
    count = SIZES[AXES.index(axis)]
    place = (lambda i, c: 2 * i + c) if axis == "z" else (lambda i, c: count * c + i)
    hops = [(place(i, c), place((i + 1 - 2 * c) % count, c)) for i in range(count) for c in range(2)]
    return lax.ppermute(block, ("z", "core") if axis == "z" else ("core", "x"), hops)


def shift(block, axis, step):
    count = SIZES[AXES.index(axis)]
    return lax.ppermute(block, axis, [(i, (i + step) % count) for i in range(count)])


def dot(left, right, left_dim, right_dim):
    return lax.dot_general(
        left, right, (((left_dim,), (right_dim,)), ((), ())), preferred_element_type=F32
    )


def later(array, other):
    across = array.shape[-1] <= other.shape[-1]
    size = (1, array.shape[-1]) if across else (array.shape[-2], 1)
    edge = lax.slice(other, (0,) * other.ndim, (1,) * (other.ndim - 2) + size).reshape(size)
    return array + (0.0 * edge.astype(F32)).astype(array.dtype)


def plus(part, received):
    return (part + received.astype(F32)).astype(BF16)


def on_device(tok, w, cot):
    yh, z, core, yl, x = (lax.axis_index(a) for a in AXES)
    sign = 1 - 2 * core

    def spot_z(other, ahead):
        return (yh + other) % 2, (z + 8 + sign * ahead) % 8

    def spot_x(other, ahead):
        return (yl + other) % 2, (x + 4 + sign * ahead) % 4

    def chip_rows(rows):
        got = swap(rows, "core")
        return jnp.where(core == 0, jnp.concatenate([rows, got], 0), jnp.concatenate([got, rows], 0))

    weights = jnp.zeros((2, 8, 192, 1536), BF16)

    def place_w(buffer, block, other, ahead):
        return lax.dynamic_update_slice(buffer, block[None, None], (*spot_z(other, ahead), 0, 0))

    across = swap(w, "yh")
    a = chip_rows(w)
    t_own = tok.T
    t_pair = jnp.concatenate([t_own, swap(t_own, "core")], 1)
    b = chip_rows(later(across, a))
    t_other = swap(later(t_own, a), "yl")
    weights = place_w(place_w(weights, a, 0, 0), b, 1, 0)
    for k in range(1, 4):
        a = ring(a, "z")
        if k == 1:
            t_other = later(t_other, a)
        weights = place_w(place_w(weights, a, 0, -k), swap(a, "core"), 0, k)
        b = ring(b, "z")
        weights = place_w(place_w(weights, b, 1, -k), swap(b, "core"), 1, k)
    last = ring(jnp.where(core == 0, a, b), "z")

    tokens, both = jnp.zeros((2, 4, 384, 512), BF16), jnp.zeros((2, 8, 96, 1024), BF16)

    def place_t(buffers, block, other, ahead, turned):
        row, column = spot_x(other, ahead)
        halves = (block[:, 512:], block[:, :512]) if turned else (block[:, :512], block[:, 512:])
        few = lax.dynamic_index_in_dim(block.reshape(2, 2, 96, 1024), core, 1, keepdims=False)
        pieces = [(few[:, :, 512:], 0), (few[:, :, :512], 512)] if turned else [(few, 0)]
        out = lax.dynamic_update_slice(buffers[0], halves[0][None, None], (row, column, 0, 0))
        part = buffers[1]
        for piece, lane in pieces:
            part = lax.dynamic_update_slice(part, piece[None], (row, 2 * column, 0, lane))
        return out, part

    a = t_pair
    b = jnp.concatenate([t_other, swap(t_other, "core")], 1)
    known = place_t(place_t((tokens, both), a, 0, 0, False), b, 1, 0, False)
    a, b = ring(a, "x"), ring(b, "x")
    known = place_t(place_t(known, a, 0, -1, False), swap(a, "core"), 0, 1, True)
    known = place_t(place_t(known, b, 1, -1, False), swap(b, "core"), 1, 1, True)
    far = ring(jnp.where(core == 0, a, b), "x")
    known = place_t(place_t(known, far, core, 2, False), swap(far, "core"), 1 - core, 2, True)

    tokens, both = known
    preact = dot(tokens.reshape(3072, 512), weights.reshape(3072, 1536), 0, 0)
    by_z = tokens.reshape(2, 8, 192, 512)
    last = later(last, preact)
    for block, other in ((last, core), (swap(last, "core"), 1 - core)):
        rows = lax.dynamic_slice(by_z, (*spot_z(other, 4), 0, 0), (1, 1, 192, 512))
        preact = preact + dot(rows.reshape(192, 512), block, 0, 0)
        weights = place_w(weights, block, other, 4)
    hidden = gelu_tanh(preact).astype(BF16)
    pull_back = jax.vjp(gelu_tanh, preact)[1]
    grad = pull_back(cot.astype(F32))[0].astype(BF16)
    grad_other = swap(grad, "core")
    grads = jnp.concatenate([grad, grad_other], 0)

    def w_rows(other, ahead):
        start = ((yh + other) % 2, (z + 8 + ahead) % 8, 0, 0)
        return lax.dynamic_slice(both, start, (1, 1, 96, 1024)).reshape(96, 1024)

    def w_parts(*found, gate=None):
        part = dot(jnp.concatenate([w_rows(*each) for each in found], 0), grads, 1, 0)
        part = part if gate is None else later(part, gate)
        return [part[96 * i : 96 * (i + 1)] for i in range(len(found))]

    def pick(array, index, other):
        return lax.dynamic_index_in_dim(array, (index + other) % 2, 0, keepdims=False)

    by_x = weights.reshape(2, 4, 384, 1536)

    def x_part(ahead, right, *gates):
        rows = lax.dynamic_index_in_dim(by_x, spot_x(0, ahead)[1], 1, keepdims=False)
        part = dot(rows, right, 2, 1)
        for gate in gates:
            part = later(part, gate)
        return part.astype(BF16)

    far = ring(x_part(2, grad), "x")

    (b_far,) = w_parts((1, 4))
    b_far = b_far.astype(BF16)
    b_up, b_down = (part.astype(BF16) for part in w_parts((1, 3), (1, -3)))
    b_up, b_down = shift(b_up, "z", 1), shift(b_down, "z", -1)
    (a_far,) = w_parts((0, 4))
    a_far = plus(a_far, swap(b_far, "yh"))
    near, near_other = x_part(1, grad, a_far), x_part(1, grad_other, a_far)
    up, down = w_parts((1, 2), (1, -2), gate=a_far)
    a_far = ring(a_far, "z")

    b_up, b_down = later(plus(up, b_up), near), later(plus(down, b_down), near_other)
    up, down = w_parts((0, 3), (0, -3), gate=b_up)
    far = later(far, b_up)
    b_up, b_down = shift(b_up, "z", 1), shift(b_down, "z", -1)
    near = ring(jnp.concatenate([plus(near.astype(F32), far), near_other], -1), "x")

    a_up = plus(up, jnp.where(core == 0, a_far, 0))
    a_down = plus(down, jnp.where(core == 1, a_far, 0))
    up, down = w_parts((1, 1), (1, -1), gate=a_up)
    a_up, a_down = shift(a_up, "z", 1), shift(a_down, "z", -1)
    home = x_part(0, grad, a_down)

    b_up, b_down = plus(up, b_up), plus(down, b_down)
    up, down = w_parts((0, 2), (0, -2), gate=b_up)
    b_up, b_down = shift(b_up, "z", 1), shift(b_down, "z", -1)

    a_up, a_down = plus(up, a_up), plus(down, a_down)
    b_home, a_home, up, down = w_parts((1, 0), (0, 0), (0, 1), (0, -1), gate=a_up)
    near = later(near, a_up)
    a_up, a_down = shift(a_up, "z", 1), shift(a_down, "z", -1)

    b_sum = plus(b_home + b_up.astype(F32), b_down)
    x_sum = home.astype(F32) + near[:, :, :512].astype(F32) + swap(near[:, :, 512:], "core").astype(F32)
    x_give = pick(x_sum, yl, 1).astype(BF16)
    a_up = later(later(plus(up, a_up), b_sum), x_give)
    a_down = later(later(plus(down, a_down), b_sum), x_give)
    b_sum, x_give = swap(b_sum, "yh"), swap(x_give, "yl")
    a_up, a_down = shift(a_up, "z", 1), shift(a_down, "z", -1)
    w_grad = plus(a_home + a_up.astype(F32) + a_down.astype(F32), b_sum)
    x_grad = plus(pick(x_sum, yl, 0), x_give).T
    return hidden, x_grad, w_grad


def solution(mesh):
    fine = Mesh(mesh.devices.reshape(SIZES), AXES)
    spec = P(("yh", "z", "core"), ("yl", "x"))
    return jax.shard_map(
        on_device, mesh=fine, in_specs=(spec,) * 3, out_specs=(spec,) * 3, check_vma=False
    )
```

```python
import jax
import jax.numpy as jnp
from jax import lax
from jax.sharding import Mesh, PartitionSpec as P

F32, BF16 = jnp.float32, jnp.bfloat16
AXES = ("yh", "z", "core", "yl", "x")
SIZES = (2, 8, 2, 2, 4)


def gelu_tanh(values):
    return jax.nn.gelu(values, approximate=True)


def swap(block, axis):
    return lax.ppermute(block, axis, [(0, 1), (1, 0)])


def ring(block, axis):
    count = SIZES[AXES.index(axis)]
    place = (lambda i, c: 2 * i + c) if axis == "z" else (lambda i, c: count * c + i)
    hops = [(place(i, c), place((i + 1 - 2 * c) % count, c)) for i in range(count) for c in range(2)]
    return lax.ppermute(block, ("z", "core") if axis == "z" else ("core", "x"), hops)


def shift(block, axis, step):
    count = SIZES[AXES.index(axis)]
    return lax.ppermute(block, axis, [(i, (i + step) % count) for i in range(count)])


def dot(left, right, left_dim, right_dim):
    return lax.dot_general(
        left, right, (((left_dim,), (right_dim,)), ((), ())), preferred_element_type=F32
    )


def later(array, other):
    across = array.shape[-1] <= other.shape[-1]
    size = (1, array.shape[-1]) if across else (array.shape[-2], 1)
    edge = lax.slice(other, (0,) * other.ndim, (1,) * (other.ndim - 2) + size).reshape(size)
    return array + (0.0 * edge.astype(F32)).astype(array.dtype)


def plus(part, received):
    return (part + received.astype(F32)).astype(BF16)


def on_device(tok, w, cot):
    yh, z, core, yl, x = (lax.axis_index(a) for a in AXES)
    sign = 1 - 2 * core

    def spot_z(other, ahead):
        return (yh + other) % 2, (z + 8 + sign * ahead) % 8

    def spot_x(other, ahead):
        return (yl + other) % 2, (x + 4 + sign * ahead) % 4

    def chip_rows(rows):
        got = swap(rows, "core")
        return jnp.where(core == 0, jnp.concatenate([rows, got], 0), jnp.concatenate([got, rows], 0))

    weights = jnp.zeros((2, 8, 192, 1536), BF16)

    def place_w(buffer, block, other, ahead):
        return lax.dynamic_update_slice(buffer, block[None, None], (*spot_z(other, ahead), 0, 0))

    across = swap(w, "yh")
    a = chip_rows(w)
    t_own = tok.T
    t_pair = jnp.concatenate([t_own, swap(t_own, "core")], 1)
    weights = place_w(weights, a, 0, 0)
    b = chip_rows(later(later(across, a), weights))
    t_other = swap(later(t_own, a), "yl")
    weights = place_w(weights, b, 1, 0)
    for k in range(1, 4):
        a = ring(a, "z")
        if k == 1:
            t_other = later(t_other, a)
        weights = place_w(place_w(weights, a, 0, -k), swap(a, "core"), 0, k)
        b = ring(b, "z")
        weights = place_w(place_w(weights, b, 1, -k), swap(b, "core"), 1, k)
    last = ring(jnp.where(core == 0, a, b), "z")

    tokens, both = jnp.zeros((2, 4, 384, 512), BF16), jnp.zeros((2, 8, 96, 1024), BF16)

    def place_t(buffers, block, other, ahead, turned):
        row, column = spot_x(other, ahead)
        halves = (block[:, 512:], block[:, :512]) if turned else (block[:, :512], block[:, 512:])
        few = lax.dynamic_index_in_dim(block.reshape(2, 2, 96, 1024), core, 1, keepdims=False)
        pieces = [(few[:, :, 512:], 0), (few[:, :, :512], 512)] if turned else [(few, 0)]
        out = lax.dynamic_update_slice(buffers[0], halves[0][None, None], (row, column, 0, 0))
        part = buffers[1]
        for piece, lane in pieces:
            part = lax.dynamic_update_slice(part, piece[None], (row, 2 * column, 0, lane))
        return out, part

    a = t_pair
    b = jnp.concatenate([t_other, swap(t_other, "core")], 1)
    known = place_t(place_t((tokens, both), a, 0, 0, False), b, 1, 0, False)
    a, b = ring(a, "x"), ring(b, "x")
    known = place_t(place_t(known, a, 0, -1, False), swap(a, "core"), 0, 1, True)
    known = place_t(place_t(known, b, 1, -1, False), swap(b, "core"), 1, 1, True)
    far = ring(jnp.where(core == 0, a, b), "x")
    known = place_t(place_t(known, far, core, 2, False), swap(far, "core"), 1 - core, 2, True)

    tokens, both = known
    preact = dot(tokens.reshape(3072, 512), weights.reshape(3072, 1536), 0, 0)
    by_z = tokens.reshape(2, 8, 192, 512)
    last = later(last, preact)
    for block, other in ((last, core), (swap(last, "core"), 1 - core)):
        rows = lax.dynamic_slice(by_z, (*spot_z(other, 4), 0, 0), (1, 1, 192, 512))
        preact = preact + dot(rows.reshape(192, 512), block, 0, 0)
        weights = place_w(weights, block, other, 4)
    hidden = gelu_tanh(preact).astype(BF16)
    pull_back = jax.vjp(gelu_tanh, preact)[1]
    grad = pull_back(cot.astype(F32))[0].astype(BF16)
    grad_other = swap(grad, "core")
    grads = jnp.concatenate([grad, grad_other], 0)

    def w_rows(other, ahead):
        start = ((yh + other) % 2, (z + 8 + ahead) % 8, 0, 0)
        return lax.dynamic_slice(both, start, (1, 1, 96, 1024)).reshape(96, 1024)

    def w_parts(*found, gate=None):
        part = dot(jnp.concatenate([w_rows(*each) for each in found], 0), grads, 1, 0)
        part = part if gate is None else later(part, gate)
        return [part[96 * i : 96 * (i + 1)] for i in range(len(found))]

    def pick(array, index, other):
        return lax.dynamic_index_in_dim(array, (index + other) % 2, 0, keepdims=False)

    by_x = weights.reshape(2, 4, 384, 1536)

    def x_part(ahead, right, *gates):
        rows = lax.dynamic_index_in_dim(by_x, spot_x(0, ahead)[1], 1, keepdims=False)
        part = dot(rows, right, 2, 1)
        for gate in gates:
            part = later(part, gate)
        return part.astype(BF16)

    far = ring(x_part(2, grad), "x")

    (b_far,) = w_parts((1, 4))
    b_far = b_far.astype(BF16)
    b_up, b_down = (part.astype(BF16) for part in w_parts((1, 3), (1, -3)))
    b_up, b_down = shift(b_up, "z", 1), shift(b_down, "z", -1)
    (a_far,) = w_parts((0, 4))
    a_far = plus(a_far, swap(b_far, "yh"))
    near, near_other = x_part(1, grad, a_far), x_part(1, grad_other, a_far)
    up, down = w_parts((1, 2), (1, -2), gate=a_far)
    a_far = ring(a_far, "z")

    b_up, b_down = later(plus(up, b_up), near), later(plus(down, b_down), near_other)
    up, down = w_parts((0, 3), (0, -3), gate=b_up)
    far = later(far, b_up)
    b_up, b_down = shift(b_up, "z", 1), shift(b_down, "z", -1)
    near = ring(jnp.concatenate([plus(near.astype(F32), far), near_other], -1), "x")

    a_up = plus(up, jnp.where(core == 0, a_far, 0))
    a_down = plus(down, jnp.where(core == 1, a_far, 0))
    up, down = w_parts((1, 1), (1, -1), gate=a_up)
    a_up, a_down = shift(a_up, "z", 1), shift(a_down, "z", -1)
    home = x_part(0, grad, a_down)

    b_up, b_down = plus(up, b_up), plus(down, b_down)
    up, down = w_parts((0, 2), (0, -2), gate=b_up)
    b_up, b_down = shift(b_up, "z", 1), shift(b_down, "z", -1)

    a_up, a_down = plus(up, a_up), plus(down, a_down)
    b_home, a_home, up, down = w_parts((1, 0), (0, 0), (0, 1), (0, -1), gate=a_up)
    near = later(near, a_up)
    a_up, a_down = shift(a_up, "z", 1), shift(a_down, "z", -1)

    b_sum = plus(b_home + b_up.astype(F32), b_down)
    x_sum = home.astype(F32) + near[:, :, :512].astype(F32) + swap(near[:, :, 512:], "core").astype(F32)
    x_give = pick(x_sum, yl, 1).astype(BF16)
    a_up = later(later(plus(up, a_up), b_sum), x_give)
    a_down = later(later(plus(down, a_down), b_sum), x_give)
    b_sum, x_give = swap(b_sum, "yh"), swap(x_give, "yl")
    a_up, a_down = shift(a_up, "z", 1), shift(a_down, "z", -1)
    w_grad = plus(a_home + a_up.astype(F32) + a_down.astype(F32), b_sum)
    x_grad = plus(pick(x_sum, yl, 0), x_give).T
    return hidden, x_grad, w_grad


def solution(mesh):
    fine = Mesh(mesh.devices.reshape(SIZES), AXES)
    spec = P(("yh", "z", "core"), ("yl", "x"))
    return jax.shard_map(
        on_device, mesh=fine, in_specs=(spec,) * 3, out_specs=(spec,) * 3, check_vma=False
    )
```
